128 devices in a mesh: bulk: 32 (over z, x_hi, y), grp: 4 (over x_lo, core).
Axes of the slice: x: 4 (x_hi: 2, x_lo: 2; x = x_hi * 2 + x_lo), y: 4, z: 4, core: 2. Of those that a mesh axis runs over, the one named last changes fastest.
Arguments:
- positions: float32 [3, 3145728], P(None, ('bulk', 'grp')), may hold values from -1 to 1
- normals: float32 [3, 3145728], P(None, ('bulk', 'grp')), may hold values from -6 to 6
- strength: float32 [3145728], P(('bulk', 'grp')), may hold values from -6 to 6
- near_index: int32 [24576, 6, 2], P(('bulk', 'grp')), may hold values from 0 to 191
- near_count: int32 [24576, 6], P(('bulk', 'grp')), may hold values from 0 to 2
Outputs:
- potential: float32 [3145728], P(('bulk', 'grp'))
The draws below stay inside these ranges and needn't reach their ends.
Inputs may be any that keep to these rules, and one draw needn't show every extreme that they name: `near_index`: indexes a block among the 192 blocks of the round's partner device.
All inputs are finite; a program needn't handle non-finite values.
Results may differ from the reference program's by a relative error of at most 0.0003.
Values sent between devices are 32-bit elements; how exact they have to be, the bound alone decides.
No kernel may reach another device: no remote copies, remote signals or barrier semaphores. Data moves between devices by JAX's collectives and lax.ppermute only.
A program may use at most 64 MiB of HBM per device.

```python
import math
import jax
import jax.numpy as jnp
import numpy as np
from jax import lax

BLK = 128
NB = 192
ROUNDS = 6
SLOTS = 2
POINTS = 3145728
BLOCKS = 24576
N_BULK = 32
N_GRP = 4


def touch_ends(entries, rng, low, top_value):
    shape = entries.shape
    place = [jax.random.randint(jax.random.fold_in(rng, axis), (), 0, shape[axis]) for axis in range(len(shape))]
    entries = entries.at[tuple(place)].set(low)
    longest = shape.index(max(shape))
    place[longest] = (place[longest] + 1) % shape[longest]
    return entries.at[tuple(place)].set(top_value)


def block_scale(key, dims, split, low, largest):
    level = 1.0
    for position, blocks in split:
        draws = jax.random.uniform(jax.random.fold_in(jax.random.fold_in(key, 6), position), (blocks,), jnp.float32, low / len(split), largest / len(split))
        level = level * jnp.repeat(jnp.exp(draws), dims[position] // blocks).reshape((-1,) + (1,) * (len(dims) - 1 - position))
    return level


def scatter_about(stream_key, shape, deviation, most, cuts=(), held_as=jnp.bfloat16):
    drawn = jax.random.normal(stream_key, shape, jnp.float32) * deviation
    if len(cuts) > 0:
        drawn = block_scale(stream_key, shape, cuts, -0.22, 0.18) * drawn
    return jnp.clip(drawn, min=-most, max=most).astype(held_as)


def setup_inputs(seed: int = 0) -> dict:
    key_list = jax.random.split(jax.random.key(seed), 6)
    return {
        "positions": jnp.clip(jax.random.uniform(key_list[0], (3, POINTS), jnp.float32, -1.0, 1.0) * block_scale(key_list[0], (3, POINTS), ((1, 128),), -0.4, 0.0), -1.0, 1.0),
        "normals": scatter_about(key_list[1], (3, POINTS), 1.0, 6.0, ((1, 128),), jnp.float32),
        "strength": scatter_about(key_list[2], (POINTS,), 1.0, 6.0, ((0, 128),), jnp.float32),
        "near_index": touch_ends(jax.random.randint(key_list[3], (BLOCKS, ROUNDS, SLOTS), 0, NB), jax.random.fold_in(key_list[3], 1), 0, NB - 1).astype(jnp.int32),
        "near_count": touch_ends(jax.random.randint(key_list[4], (BLOCKS, ROUNDS), 0, SLOTS + 1), jax.random.fold_in(key_list[4], 1), 0, SLOTS).astype(jnp.int32),
    }


DELTA2 = 0.05

def tile_sum(targets, src_pos, src_nrm, src_q):
    high = lax.Precision.HIGHEST
    cross = targets[0][:, None, :, None] * src_pos[0][:, :, None, :]
    normal_dot = targets[0][:, None, :, None] * src_nrm[0][:, :, None, :]
    for comp in range(1, 3):
        cross = cross + targets[comp][:, None, :, None] * src_pos[comp][:, :, None, :]
        normal_dot = normal_dot + targets[comp][:, None, :, None] * src_nrm[comp][:, :, None, :]
    target_sq = lax.optimization_barrier(jnp.sum(targets * targets, axis=0))
    source_sq = lax.optimization_barrier(jnp.sum(src_pos * src_pos, axis=0))
    source_nd = lax.optimization_barrier(jnp.sum(src_pos * src_nrm, axis=0))
    dist = target_sq[:, None, :, None] + source_sq[:, :, None, :] - 2.0 * cross + DELTA2
    kernel = (normal_dot - source_nd[:, :, None, :]) * lax.rsqrt(dist) / dist
    return jnp.einsum('tkij,tkj->tki', kernel, src_q, precision=high) * (1.0 / (4.0 * math.pi))

def reference(positions, normals, strength, near_index, near_count):
    devices = N_BULK * N_GRP
    pos_all = positions.reshape(3, devices * NB, BLK)
    nrm_all = normals.reshape(3, devices * NB, BLK)
    q_all = strength.reshape(devices * NB, BLK)
    index_all = near_index.reshape(devices, NB, ROUNDS * SLOTS)
    count_all = near_count.reshape(devices, NB, ROUNDS)
    masks = [1, 2, N_GRP, 2 * N_GRP, 4 * N_GRP, N_BULK // 2 * N_GRP]
    table = np.stack([np.arange(devices) ^ m for m in masks], 1).astype(np.int32)
    partners = jnp.asarray(table, jnp.int32)

    def one_device(dev):
        start = (dev * NB).astype(jnp.int32)
        targets = lax.dynamic_slice_in_dim(pos_all, start, NB, 1)
        own_n = lax.dynamic_slice_in_dim(nrm_all, start, NB, 1)
        own_q = lax.dynamic_slice_in_dim(q_all, start, NB, 0)
        total = tile_sum(targets, targets[:, :, None, :], own_n[:, :, None, :], own_q[:, None, :])[:, 0]
        owners = jnp.repeat(partners[dev], SLOTS)
        global_ids = (owners[None, :] * NB + index_all[dev]).astype(jnp.int32)
        src_pos = pos_all[:, global_ids]
        src_nrm = nrm_all[:, global_ids]
        src_q = q_all[global_ids]
        slot_ids = jnp.arange(SLOTS, dtype=jnp.int32)
        weight = (slot_ids[None, None, :] < count_all[dev][:, :, None]).astype(jnp.float32)
        weight = weight.reshape(NB, ROUNDS * SLOTS)
        parts = tile_sum(targets, src_pos, src_nrm, src_q)
        return total + lax.optimization_barrier(jnp.sum(parts * weight[:, :, None], axis=1))
    result = lax.map(one_device, jnp.arange(devices, dtype=jnp.int32))
    return result.reshape(-1)
```

```python
import functools
import math

import jax
import jax.numpy as jnp
from jax import lax
from jax.experimental import pallas as pl
from jax.experimental.pallas import tpu as pltpu
from jax.sharding import PartitionSpec as P

DELTA2 = 0.05
BLK = 128
U = 32
KF = 32


def from_partner(x, axis, stride):
    return lax.ppermute(x, axis, [(i, i ^ 1 << stride) for i in range(lax.axis_size(axis))])


def split3(v):
    h = v.astype(jnp.bfloat16).astype(jnp.float32)
    r = v - h
    m = r.astype(jnp.bfloat16).astype(jnp.float32)
    return h, m, r - m


def row(ref, c, b):
    return jnp.broadcast_to(ref[c, pl.ds(b, 1), :], (8, BLK))


def by_row(sub, a, b, c, d):
    k = sub & 3
    return jnp.where(k == 0, a, jnp.where(k == 1, b, jnp.where(k == 2, c, d)))


def target_features(msg, b, sub):
    x, y, z = row(msg, 0, b), row(msg, 1, b), row(msg, 2, b)
    h, m, l = split3(by_row(sub, x, y, z, x * x + y * y + z * z + DELTA2))
    last, low = (sub & 3) == 3, sub < 4
    h1 = jnp.where(last, 1.0, h)
    bands = [h1, jnp.where(low, h1, jnp.where(last, h, m)), jnp.where(low, m, l), jnp.zeros_like(h)]
    return jnp.concatenate(bands, axis=0)


def source_bands(v, sub, unit):
    h, m, l = split3(v)
    last, low = (sub & 3) == 3, sub < 4
    hu = jnp.where(last, unit, h)
    mu = jnp.where(last, unit, m)
    bands = [jnp.where(low, h, m), jnp.where(low, l, hu), jnp.where(low, mu, hu), jnp.zeros_like(h)]
    return jnp.concatenate(bands, axis=0).astype(jnp.bfloat16)


def source_features(msg, b, sub):
    x, y, z = row(msg, 0, b), row(msg, 1, b), row(msg, 2, b)
    u, v, w = row(msg, 3, b), row(msg, 4, b), row(msg, 5, b)
    dist = by_row(sub, -2.0 * x, -2.0 * y, -2.0 * z, x * x + y * y + z * z)
    num = by_row(sub, u, v, w, -(x * u + y * v + z * w))
    return source_bands(dist, sub, 1.0), source_bands(num, sub, 0.0)


def phase_kernel(nb, rounds, own, last, index, count, *refs):
    n_src = len(rounds) + (1 if own else 0)
    mine = refs[0]
    msgs = refs[:1] if own else ()
    msgs = tuple(msgs) + tuple(refs[1:1 + len(rounds)])
    rest = refs[1 + len(rounds):]
    if not own:
        before, rest = rest[0], rest[1:]
    out, left, right, acc, work = rest

    sub = lax.broadcasted_iota(jnp.int32, (8, BLK), 0)
    lane = lax.broadcasted_iota(jnp.int32, (8, BLK), 1)
    group = lane >> 3

    if own:
        acc[...] = jnp.zeros_like(acc)
    else:
        acc[pl.ds(0, nb)] = before[...]
    left[pl.ds(nb * BLK, BLK), :] = jnp.zeros((BLK, BLK), jnp.bfloat16)

    def build_left(b, _):
        f = target_features(mine, b, sub)
        left[pl.ds(pl.multiple_of(b * BLK, BLK), BLK), :KF] = f.T.astype(jnp.bfloat16)
        return 0

    lax.fori_loop(0, nb, build_left, 0, unroll=4)

    n = jnp.int32(0)
    for k, msg in enumerate(msgs):
        r = -1 if own and k == 0 else rounds[k - (1 if own else 0)]

        def build_right(b, n, msg=msg, k=k, r=r):
            d, f = source_features(msg, b, sub)
            right[k * nb + b, :, :BLK] = d
            right[k * nb + b, :, BLK:] = f
            if r < 0:
                work[n] = (b << 12) + b
                return n + 1
            c = count[r * nb + b]
            base = (b << 12) + k * nb
            work[n] = base + index[(2 * r) * nb + b]
            work[n + 1] = base + index[(2 * r + 1) * nb + b]
            return n + c

        n = lax.fori_loop(0, nb, build_right, n, unroll=4)

    for u in range(U):
        work[n + u] = jnp.int32(nb << 12)

    def tiles(i, _):
        codes = [work[i * U + u] for u in range(U)]
        prods = []
        for code in codes:
            a = left[pl.ds(pl.multiple_of((code >> 12) * BLK, BLK), BLK), :KF]
            prods.append(jnp.dot(a, right[code & 4095], preferred_element_type=jnp.float32))
        for code, p in zip(codes, prods):
            s = lax.rsqrt(p[:, :BLK])
            w = p[:, BLK:] * (s * (s * s))
            total = jnp.broadcast_to(jnp.sum(w, axis=1, keepdims=True), (BLK, BLK)).reshape(16, 8, BLK)
            a = total[0]
            for g in range(1, 16):
                a = jnp.where(group == g, total[g], a)
            acc[code >> 12] += a
        return 0

    lax.fori_loop(0, (n + U - 1) // U, tiles, 0)

    if last:
        keep = (lane & 7) == sub

        def finish(i, _):
            a = acc[pl.ds(i * 8, 8)]
            out[pl.ds(pl.multiple_of(i * 8, 8), 8), :] = jnp.sum(jnp.where(keep[None], a, 0.0), axis=1)
            return 0

        lax.fori_loop(0, nb // 8, finish, 0)
    else:
        out[...] = acc[pl.ds(0, nb)]


def phase(name, rounds, own, last, index, count, mine, msgs, before):
    nb = mine.shape[1]
    n_src = len(rounds) + (1 if own else 0)
    smem, vmem = pl.BlockSpec(memory_space=pltpu.SMEM), pl.BlockSpec(memory_space=pltpu.VMEM)
    args = [index, count, mine, *msgs] + ([] if own else [before])
    shape = (nb, BLK) if last else (nb, 8, BLK)
    return pl.pallas_call(
        functools.partial(phase_kernel, nb, tuple(rounds), own, last),
        out_shape=jax.ShapeDtypeStruct(shape, jnp.float32),
        in_specs=[smem, smem] + [vmem] * (len(args) - 2),
        out_specs=vmem,
        scratch_shapes=[
            pltpu.VMEM(((nb + 1) * BLK, BLK), jnp.bfloat16),
            pltpu.VMEM((n_src * nb, KF, 2 * BLK), jnp.bfloat16),
            pltpu.VMEM((nb + 1, 8, BLK), jnp.float32),
            pltpu.SMEM((n_src * 2 * nb + 2 * U,), jnp.int32),
        ],
        compiler_params=pltpu.CompilerParams(vmem_limit_bytes=40 << 20),
        cost_estimate=pl.CostEstimate(flops=n_src * 2_000_000_000, bytes_accessed=n_src * 1_000_000, transcendentals=0),
        name=name,
    )(*args)


def shards(positions, normals, strength, near_index, near_count):
    nb = near_index.shape[0]
    scaled = normals * (strength * (1.0 / (4.0 * math.pi)))[None]
    mine = jnp.concatenate([positions, scaled], axis=0).reshape(6, nb, BLK)
    top_bit = lax.axis_size("bulk").bit_length() - 2
    plan = [("grp", 0), ("grp", 1), ("bulk", 0), ("bulk", 1), ("bulk", 2), ("bulk", top_bit)]
    far = [from_partner(mine, axis, bit) for axis, bit in plan]
    index = near_index.transpose(1, 2, 0).reshape(-1)
    count = near_count.T.reshape(-1)
    a = phase("own_core", [0], True, False, index, count, mine, [far[0]], None)
    b = phase("mid", [5, 1, 2], False, False, index, count, mine, [far[5], far[1], far[2]], a)
    c = phase("end", [3, 4], False, True, index, count, mine, [far[3], far[4]], b)
    return c.reshape(-1)


def solution(mesh):
    in_specs = (
        P(None, ("bulk", "grp")),
        P(None, ("bulk", "grp")),
        P(("bulk", "grp")),
        P(("bulk", "grp"), None, None),
        P(("bulk", "grp"), None),
    )
    out_specs = P(("bulk", "grp"))
    return jax.shard_map(shards, mesh=mesh, in_specs=in_specs, out_specs=out_specs, check_vma=False)
```

```python
import functools
import math

import jax
import jax.numpy as jnp
from jax import lax
from jax.experimental import pallas as pl
from jax.experimental.pallas import tpu as pltpu
from jax.sharding import PartitionSpec as P

DELTA2 = 0.05
BLK = 128
U = 48
KF = 48
STEPS = 3
PAD = 64


def from_partner(x, axis, stride):
    return lax.ppermute(x, axis, [(i, i ^ 1 << stride) for i in range(lax.axis_size(axis))])


def split3(v):
    h = v.astype(jnp.bfloat16).astype(jnp.float32)
    r = v - h
    m = r.astype(jnp.bfloat16).astype(jnp.float32)
    return h, m, r - m


def row(msg, c, nb, b):
    return jnp.broadcast_to(msg[pl.ds(c * nb + b, 1), :], (8, BLK))


def target_features(msg, nb, b, sub):
    x, y, z = row(msg, 0, nb, b), row(msg, 1, nb, b), row(msg, 2, nb, b)
    k = jnp.where(sub < 3, sub, sub - 3)
    v = jnp.where(k == 0, x, jnp.where(k == 1, y, z))
    h, m, l = split3(jnp.where(sub < 6, v, x * x + y * y + z * z + DELTA2))
    for_dist = jnp.where(sub < 3, -2.0, 0.0)
    for_num = jnp.where((sub >= 3) & (sub < 6), 1.0, 0.0)
    six = jnp.where(sub == 6, 1.0, 0.0)
    seven = jnp.where(sub == 7, -1.0, 0.0)
    dh, dm, dl = h * for_dist + six, m * for_dist, l * (for_dist + six)
    nh, nm, nl = h * for_num + seven, m * for_num, l * for_num
    dist = jnp.concatenate([dh, dh, dh, dm + h * six, dm + m * six, dl], axis=0)
    num = jnp.concatenate([nh, nh, nh, nm, nm, nl], axis=0)
    return jnp.concatenate([dist, num], axis=1).astype(jnp.bfloat16)


def source_features(msg, nb, b, sub):
    x, y, z = row(msg, 0, nb, b), row(msg, 1, nb, b), row(msg, 2, nb, b)
    u, v, w = row(msg, 3, nb, b), row(msg, 4, nb, b), row(msg, 5, nb, b)
    six = msg[pl.ds(b, 6, stride=nb), :]
    six = jnp.concatenate([six, jnp.zeros((2, BLK), jnp.float32)], axis=0)
    f = jnp.where(sub == 6, x * x + y * y + z * z, jnp.where(sub == 7, x * u + y * v + z * w, six))
    h, m, l = split3(f)
    hu = jnp.where(sub < 6, h, 1.0)
    mu = jnp.where(sub < 6, m, 1.0)
    return jnp.concatenate([h, m, l, hu, mu, hu], axis=0)


def phase_kernel(nb, rounds, own, last, lists, sizes, *refs):
    n_src = len(rounds) + (1 if own else 0)
    n_msg = n_src
    msgs, refs = refs[:n_msg], refs[n_msg:]
    if own:
        out, tgt, refs = refs[0], refs[1], refs[2:]
    else:
        before, tgt, out, refs = refs[0], refs[1], refs[2], refs[3:]
    even, odd, acc = refs
    src = (even, odd)
    width = 2 * nb + PAD
    ids = ([6] if own else []) + list(rounds)

    sub = lax.broadcasted_iota(jnp.int32, (8, BLK), 0)

    if own:
        acc[...] = jnp.zeros_like(acc)
        tgt[nb] = jnp.zeros((KF, 2 * BLK), jnp.bfloat16)
    else:
        acc[pl.ds(0, nb)] = before[...]

    def build(k, b):
        msg = msgs[k]
        f = source_features(msg, nb, b, sub)
        start = pl.multiple_of((k // 2 * nb + b) * BLK, BLK)
        src[k % 2][pl.ds(start, BLK), :KF] = f.astype(jnp.bfloat16).T
        if own and k == 0:
            tgt[b] = target_features(msg, nb, b, sub)

    def code_at(par, p):
        mine = ids[par::2]
        here = mine[0] * width + p
        if len(mine) > 1:
            size = sizes[mine[0]]
            here = jnp.where(p < size, here, mine[1] * width + (p - size))
        return lists[here]

    def tiles(par, at, ready, between):
        codes = []
        for u in range(U):
            code = code_at(par, at + u)
            codes.append(code if ready is None else jnp.where(ready, code, nb << 12))
        prods = []
        for code in codes:
            a = src[par][pl.ds(pl.multiple_of((code & 4095) * BLK, BLK), BLK), :KF]
            prods.append(jnp.dot(a, tgt[code >> 12], preferred_element_type=jnp.float32))
        between()
        for code, p in zip(codes, prods):
            s = lax.rsqrt(p[:, :BLK])
            w = p[:, BLK:] * (s * (s * s))
            acc[code >> 12] += jnp.sum(w.reshape(16, 8, BLK), axis=0)

    step = nb // STEPS

    def make(k, i):
        for j in range(step):
            build(k, i * step + j)

    def first(i, _):
        make(0, i)
        return 0

    lax.fori_loop(0, STEPS, first, 0)
    found = [sizes[ids[0]], jnp.int32(0)]
    done = [jnp.int32(0), jnp.int32(0)]
    for k in range(1, n_src):
        par = (k - 1) % 2

        def both(i, at, k=k, par=par, have=found[par]):
            ready = at + U <= have
            tiles(par, at, ready, lambda: make(k, i))
            return jnp.where(ready, at + U, at)

        done[par] = lax.fori_loop(0, STEPS, both, done[par])
        found[k % 2] += sizes[ids[k]]

    for par in range(min(2, n_src)):

        def rest(i, at, par=par):
            tiles(par, at, None, lambda: None)
            return at + U

        lax.fori_loop(0, (found[par] - done[par] + U - 1) // U, rest, done[par])

    if last:

        def finish(i, _):
            out[pl.ds(pl.multiple_of(i * 8, 8), 8), :] = jnp.sum(acc[pl.ds(i * 8, 8)], axis=1)
            return 0

        lax.fori_loop(0, nb // 8, finish, 0)
    else:
        out[...] = acc[pl.ds(0, nb)]


def phase(name, rounds, own, last, lists, sizes, msgs, before):
    nb = msgs[0].shape[0] // 6
    n_src = len(msgs)
    smem, vmem = pl.BlockSpec(memory_space=pltpu.SMEM), pl.BlockSpec(memory_space=pltpu.VMEM)
    args = [lists, sizes, *msgs, *before]
    shapes = [jax.ShapeDtypeStruct((nb, BLK) if last else (nb, 8, BLK), jnp.float32)]
    if own:
        shapes.append(jax.ShapeDtypeStruct((nb + 1, KF, 2 * BLK), jnp.bfloat16))
    return pl.pallas_call(
        functools.partial(phase_kernel, nb, tuple(rounds), own, last),
        out_shape=shapes,
        in_specs=[smem, smem] + [vmem] * (len(args) - 2),
        out_specs=[vmem] * len(shapes),
        scratch_shapes=[
            pltpu.VMEM(((n_src + 1) // 2 * nb * BLK, BLK), jnp.bfloat16),
            pltpu.VMEM((n_src // 2 * nb * BLK, BLK), jnp.bfloat16),
            pltpu.VMEM((nb + 1, 8, BLK), jnp.float32),
        ],
        compiler_params=pltpu.CompilerParams(vmem_limit_bytes=40 << 20),
        cost_estimate=pl.CostEstimate(flops=n_src * 2_000_000_000, bytes_accessed=n_src * 1_000_000, transcendentals=0),
        name=name,
    )(*args)


def tile_lists(near_index, near_count):
    nb, rounds, slots = near_index.shape
    width = slots * nb + PAD
    half = [0, 0, 1, 0, 0, 0]
    t = jnp.arange(nb, dtype=jnp.int32)
    place = jnp.arange(width, dtype=jnp.int32)
    count = near_count.T
    index = near_index.transpose(1, 2, 0)
    before = jnp.sum(jnp.where(t[:, None] < t[None, :], count[:, :, None], 0), axis=1)
    size = jnp.sum(count, axis=1)
    lists = jnp.where(place[None] < size[:, None], 0, nb << 12)
    for s in range(slots):
        code = index[:, s] + (t << 12) + (jnp.array(half, jnp.int32) * nb)[:, None]
        at = jnp.where(s < count, before + s, -1)
        lists += jnp.sum(jnp.where(at[:, :, None] == place, code[:, :, None], 0), axis=1)
    own = jnp.where(place < nb, (place << 12) + place, nb << 12)
    lists = jnp.concatenate([lists, own[None]], axis=0).reshape(-1)
    return lists, jnp.concatenate([size, jnp.full((1,), nb, jnp.int32)])


def shards(positions, normals, strength, near_index, near_count):
    nb = near_index.shape[0]
    scaled = normals * (strength * (1.0 / (4.0 * math.pi)))[None]
    mine = jnp.concatenate([positions, scaled], axis=0).reshape(6 * nb, BLK)
    top_bit = lax.axis_size("bulk").bit_length() - 2
    plan = [("grp", 0), ("grp", 1), ("bulk", 0), ("bulk", 1), ("bulk", 2), ("bulk", top_bit)]
    far = [from_partner(mine, axis, bit) for axis, bit in plan]
    lists, sizes = tile_lists(near_index, near_count)
    a, tgt = phase("own_core", [0], True, False, lists, sizes, [mine, far[0]], [])
    (b,) = phase("mid", [5, 1, 2], False, False, lists, sizes, [far[5], far[1], far[2]], [a, tgt])
    (c,) = phase("end", [3, 4], False, True, lists, sizes, [far[3], far[4]], [b, tgt])
    return c.reshape(-1)


def solution(mesh):
    in_specs = (
        P(None, ("bulk", "grp")),
        P(None, ("bulk", "grp")),
        P(("bulk", "grp")),
        P(("bulk", "grp"), None, None),
        P(("bulk", "grp"), None),
    )
    out_specs = P(("bulk", "grp"))
    return jax.shard_map(shards, mesh=mesh, in_specs=in_specs, out_specs=out_specs, check_vma=False)
```

```python
import functools
import math

import jax
import jax.numpy as jnp
from jax import lax
from jax.experimental import pallas as pl
from jax.experimental.pallas import tpu as pltpu
from jax.sharding import PartitionSpec as P

DELTA2 = 0.05
BLK = 128
U = 48
KF = 48
STEPS = 3
PAD = 128
OWN = 6


def from_partner(x, axis, stride):
    return lax.ppermute(x, axis, [(i, i ^ 1 << stride) for i in range(lax.axis_size(axis))])


def split3(v):
    h = v.astype(jnp.bfloat16).astype(jnp.float32)
    r = v - h
    m = r.astype(jnp.bfloat16).astype(jnp.float32)
    return h, m, r - m


def row(msg, c, nb, b):
    return jnp.broadcast_to(msg[pl.ds(c * nb + b, 1), :], (8, BLK))


def target_features(msg, nb, b, sub):
    x, y, z = row(msg, 0, nb, b), row(msg, 1, nb, b), row(msg, 2, nb, b)
    k = jnp.where(sub < 3, sub, sub - 3)
    v = jnp.where(k == 0, x, jnp.where(k == 1, y, z))
    h, m, l = split3(jnp.where(sub < 6, v, x * x + y * y + z * z + DELTA2))
    for_dist = jnp.where(sub < 3, -2.0, 0.0)
    for_num = jnp.where((sub >= 3) & (sub < 6), 1.0, 0.0)
    six = jnp.where(sub == 6, 1.0, 0.0)
    seven = jnp.where(sub == 7, -1.0, 0.0)
    dh, dm, dl = h * for_dist + six, m * for_dist, l * (for_dist + six)
    nh, nm, nl = h * for_num + seven, m * for_num, l * for_num
    dist = jnp.concatenate([dh, dh, dh, dm + h * six, dm + m * six, dl], axis=0)
    num = jnp.concatenate([nh, nh, nh, nm, nm, nl], axis=0)
    return jnp.concatenate([dist, num], axis=1).astype(jnp.bfloat16)


def source_features(msg, nb, b, sub):
    x, y, z = row(msg, 0, nb, b), row(msg, 1, nb, b), row(msg, 2, nb, b)
    u, v, w = row(msg, 3, nb, b), row(msg, 4, nb, b), row(msg, 5, nb, b)
    six = msg[pl.ds(b, 6, stride=nb), :]
    six = jnp.concatenate([six, jnp.zeros((2, BLK), jnp.float32)], axis=0)
    f = jnp.where(sub == 6, x * x + y * y + z * z, jnp.where(sub == 7, x * u + y * v + z * w, six))
    h, m, l = split3(f)
    hu = jnp.where(sub < 6, h, 1.0)
    mu = jnp.where(sub < 6, m, 1.0)
    return jnp.concatenate([h, m, l, hu, mu, hu], axis=0)


def phase_kernel(nb, chain, carry_in, carry_out, last, lists, *refs):
    own = not carry_in
    n = len(chain)
    n_msg = n - (1 if carry_in else 0)
    msgs, refs = refs[:n_msg], refs[n_msg:]
    if own:
        out, tgt, refs = refs[0], refs[1], refs[2:]
    else:
        before, tgt, src_in, out, refs = refs[0], refs[1], refs[2], refs[3], refs[4:]
    if carry_out:
        src_out, refs = refs[0], refs[1:]
    acc, kept = refs[0], list(refs[1:])
    src = ([src_in] if carry_in else []) + kept + ([src_out] if carry_out else [])
    width = 2 * nb + PAD
    sizes = [lists[7 * width + i] for i in chain]
    sub = lax.broadcasted_iota(jnp.int32, (8, BLK), 0)

    if own:
        acc[...] = jnp.zeros_like(acc)
        tgt[nb] = jnp.zeros((KF, 2 * BLK), jnp.bfloat16)
    else:
        acc[pl.ds(0, nb)] = before[...]

    step = nb // STEPS

    def make(k, i):
        msg = msgs[k - (1 if carry_in else 0)]
        for j in range(step):
            b = i * step + j
            f = source_features(msg, nb, b, sub)
            src[k][pl.ds(pl.multiple_of(b * BLK, BLK), BLK), :KF] = f.astype(jnp.bfloat16).T
            if chain[k] == OWN:
                tgt[b] = target_features(msg, nb, b, sub)

    def tiles(slots, between):
        codes, prods = [], []
        for k, p in slots:
            codes.append(lists[chain[k] * width + p])
        for (k, _), code in zip(slots, codes):
            a = src[k][pl.ds(pl.multiple_of((code & 255) * BLK, BLK), BLK), :KF]
            prods.append(jnp.dot(a, tgt[code >> 12], preferred_element_type=jnp.float32))
        between()
        for code, p in zip(codes, prods):
            s = lax.rsqrt(p[:, :BLK])
            w = p[:, BLK:] * (s * (s * s))
            acc[code >> 12] += jnp.sum(w.reshape(16, 8, BLK), axis=0)

    if own:

        def first(i, _):
            make(0, i)
            return 0

        lax.fori_loop(0, STEPS, first, 0)

    done = [jnp.int32(0)] * n
    for k in range(1, n):

        def both(i, at, k=k):
            ready = at + U <= sizes[k - 1]
            at_or_none = jnp.where(ready, at, width - U)
            tiles([(k - 1, at_or_none + u) for u in range(U)], lambda: make(k, i))
            return jnp.where(ready, at + U, at)

        done[k - 1] = lax.fori_loop(0, STEPS, both, done[k - 1])

    groups = [list(range(n - 1))] + ([] if carry_out else [[n - 1]])
    for group in groups:
        each = U // len(group)
        todo = jnp.int32(0)
        for k in group:
            todo = jnp.maximum(todo, (sizes[k] - done[k] + each - 1) // each)

        def rest(i, at, group=group, each=each):
            slots = [(k, jnp.minimum(p + u, width - 1)) for k, p in zip(group, at) for u in range(each)]
            tiles(slots, lambda: None)
            return tuple(p + each for p in at)

        lax.fori_loop(0, todo, rest, tuple(done[k] for k in group))

    if last:

        def finish(i, _):
            out[pl.ds(pl.multiple_of(i * 8, 8), 8), :] = jnp.sum(acc[pl.ds(i * 8, 8)], axis=1)
            return 0

        lax.fori_loop(0, nb // 8, finish, 0, unroll=4)
    else:
        out[...] = acc[pl.ds(0, nb)]


def phase(name, chain, lists, msgs, before, carry_out):
    nb = msgs[0].shape[0] // 6
    carry_in = len(before) > 0
    last = not carry_out
    smem, vmem = pl.BlockSpec(memory_space=pltpu.SMEM), pl.BlockSpec(memory_space=pltpu.VMEM)
    args = [lists, *msgs, *before]
    shapes = [jax.ShapeDtypeStruct((nb, BLK) if last else (nb, 8, BLK), jnp.float32)]
    if not carry_in:
        shapes.append(jax.ShapeDtypeStruct((nb + 1, KF, 2 * BLK), jnp.bfloat16))
    if carry_out:
        shapes.append(jax.ShapeDtypeStruct((nb * BLK, BLK), jnp.bfloat16))
    kept = len(chain) - (1 if carry_in else 0) - (1 if carry_out else 0)
    return pl.pallas_call(
        functools.partial(phase_kernel, nb, tuple(chain), carry_in, carry_out, last),
        out_shape=shapes,
        in_specs=[smem] + [vmem] * (len(args) - 1),
        out_specs=[vmem] * len(shapes),
        scratch_shapes=[pltpu.VMEM((nb + 1, 8, BLK), jnp.float32)] + [pltpu.VMEM((nb * BLK, BLK), jnp.bfloat16)] * kept,
        compiler_params=pltpu.CompilerParams(vmem_limit_bytes=26 << 20),
        cost_estimate=pl.CostEstimate(
            flops=len(chain) * 2_000_000_000, bytes_accessed=len(chain) * 1_000_000, transcendentals=0
        ),
        name=name,
    )(*args)


def start_kernel(nb, rounds, *refs):
    outside, (msg, lists), inside, sems = refs[:5], refs[5:7], refs[7:12], refs[12]
    copies = [pltpu.make_async_copy(o, i, sems.at[n]) for n, (o, i) in enumerate(zip(outside, inside))]
    for copy in copies[::-1]:
        copy.start()
    pos, nrm, dens, index, count = inside

    def plane(i, _):
        for j in range(8):
            b = i * 8 + j
            at = pl.ds(pl.multiple_of(b * BLK, BLK), BLK)
            msg[pl.ds(b, 3, stride=nb), :] = pos[:, at]
            q = dens[pl.ds(b, 1), :] * (1.0 / (4.0 * math.pi))
            msg[pl.ds(3 * nb + b, 3, stride=nb), :] = nrm[:, at] * q
        return 0

    copies[4].wait()
    copies[3].wait()
    width = 2 * nb + PAD
    slots = index.shape[1]
    c = count[...]
    t_row = lax.broadcasted_iota(jnp.int32, (nb, nb), 0)
    t_col = lax.broadcasted_iota(jnp.int32, (nb, nb), 1)
    earlier = jnp.where(t_row < t_col, 1.0, 0.0).astype(jnp.bfloat16)
    pad = jnp.zeros((16 - rounds, nb), jnp.float32)
    cf = jnp.concatenate([c.astype(jnp.float32), pad], axis=0)
    before = jnp.dot(cf.astype(jnp.bfloat16), earlier, preferred_element_type=jnp.float32)
    size = jnp.sum(cf, axis=1, keepdims=True)
    place = lax.broadcasted_iota(jnp.int32, (1, width), 1)
    spot = lax.broadcasted_iota(jnp.int32, (width, nb), 0).astype(jnp.float32)
    t = lax.broadcasted_iota(jnp.int32, (1, nb), 1).astype(jnp.float32)
    rest = jnp.zeros((14, nb), jnp.float32)
    rows = []
    for r in range(rounds):
        both = jnp.zeros((16, width), jnp.float32)
        for s in range(slots):
            at = jnp.where(cf[r:r + 1] > s, before[r:r + 1] + s, -1.0)
            hot = jnp.where(spot == at, 1.0, 0.0).astype(jnp.bfloat16)
            code = jnp.concatenate([index[r, pl.ds(s, 1), :].astype(jnp.float32), t, rest], axis=0)
            both += lax.dot_general(
                code.astype(jnp.bfloat16), hot, (((1,), (1,)), ((), ())), preferred_element_type=jnp.float32
            )
        row = (both[1:2] * 4096.0 + both[0:1]).astype(jnp.int32)
        rows.append(jnp.where(place.astype(jnp.float32) < size[r:r + 1], row, nb << 12))
    rows.append(jnp.where(place < nb, (place << 12) + place, nb << 12))
    sub = lax.broadcasted_iota(jnp.int32, (16, BLK), 0)
    lane = lax.broadcasted_iota(jnp.int32, (16, BLK), 1)
    sizes = jnp.sum(jnp.where(sub == lane, size, 0.0), axis=0, keepdims=True)
    sizes = jnp.where(lane[:1] == rounds, float(nb), sizes).astype(jnp.int32)
    parts = width // BLK
    for i, row in enumerate(rows):
        for q in range(parts):
            lists[pl.ds(i * parts + q, 1), :] = row[:, q * BLK:(q + 1) * BLK]
    lists[pl.ds(len(rows) * parts, 1), :] = sizes
    for copy in copies[:3]:
        copy.wait()
    lax.fori_loop(0, nb // 8, plane, 0)


def start(positions, normals, strength, near_index, near_count):
    nb, rounds, slots = near_index.shape
    rows = (rounds + 2) * (slots * nb + PAD) // BLK
    vmem = pl.BlockSpec(memory_space=pltpu.VMEM)
    index = near_index.transpose(1, 2, 0)
    args = [positions, normals, strength.reshape(nb, BLK), index, near_count.T]
    msg, lists = pl.pallas_call(
        functools.partial(start_kernel, nb, rounds),
        out_shape=[
            jax.ShapeDtypeStruct((6 * nb, BLK), jnp.float32),
            jax.ShapeDtypeStruct((rows, BLK), jnp.int32),
        ],
        in_specs=[pl.BlockSpec(memory_space=pltpu.HBM)] * 5,
        out_specs=[vmem] * 2,
        scratch_shapes=[pltpu.VMEM(a.shape, a.dtype) for a in args] + [pltpu.SemaphoreType.DMA((5,))],
        compiler_params=pltpu.CompilerParams(vmem_limit_bytes=24 << 20),
        name="start",
    )(*[pltpu.with_memory_space_constraint(a, pltpu.HBM) for a in args])
    return msg, lists.reshape(-1)


def shards(positions, normals, strength, near_index, near_count):
    mine, lists = start(positions, normals, strength, near_index, near_count)
    top_bit = lax.axis_size("bulk").bit_length() - 2
    plan = [("grp", 0), ("grp", 1), ("bulk", 0), ("bulk", 1), ("bulk", 2), ("bulk", top_bit)]
    far = [from_partner(mine, axis, bit) for axis, bit in plan]
    a, tgt, held = phase("own_core", [OWN, 0], lists, [mine, far[0]], [], True)
    b, held = phase("mid", [0, 5, 1, 2], lists, [far[5], far[1], far[2]], [a, tgt, held], True)
    (c,) = phase("end", [2, 3, 4], lists, [far[3], far[4]], [b, tgt, held], False)
    return c.reshape(-1)


def solution(mesh):
    in_specs = (
        P(None, ("bulk", "grp")),
        P(None, ("bulk", "grp")),
        P(("bulk", "grp")),
        P(("bulk", "grp"), None, None),
        P(("bulk", "grp"), None),
    )
    out_specs = P(("bulk", "grp"))
    return jax.shard_map(shards, mesh=mesh, in_specs=in_specs, out_specs=out_specs, check_vma=False)
```

```python
import functools
import math

import jax
import jax.numpy as jnp
from jax import lax
from jax.experimental import pallas as pl
from jax.experimental.pallas import tpu as pltpu
from jax.sharding import PartitionSpec as P

DELTA2 = 0.05
BLK = 128
U = 52
KF = 48
STEPS = 4
PAD = 128
OWN = 6


def from_partner(x, axis, stride):
    return lax.ppermute(x, axis, [(i, i ^ 1 << stride) for i in range(lax.axis_size(axis))])


def split3(v):
    h = v.astype(jnp.bfloat16).astype(jnp.float32)
    r = v - h
    m = r.astype(jnp.bfloat16).astype(jnp.float32)
    return h, m, r - m


def row(msg, c, nb, b):
    return jnp.broadcast_to(msg[pl.ds(c * nb + b, 1), :], (8, BLK))


def target_features(msg, nb, b, sub):
    x, y, z = row(msg, 0, nb, b), row(msg, 1, nb, b), row(msg, 2, nb, b)
    k = jnp.where(sub < 3, sub, sub - 3)
    v = jnp.where(k == 0, x, jnp.where(k == 1, y, z))
    h, m, l = split3(jnp.where(sub < 6, v, x * x + y * y + z * z + DELTA2))
    for_dist = jnp.where(sub < 3, -2.0, 0.0)
    for_num = jnp.where((sub >= 3) & (sub < 6), 1.0, 0.0)
    six = jnp.where(sub == 6, 1.0, 0.0)
    seven = jnp.where(sub == 7, -1.0, 0.0)
    dh, dm, dl = h * for_dist + six, m * for_dist, l * (for_dist + six)
    nh, nm, nl = h * for_num + seven, m * for_num, l * for_num
    dist = jnp.concatenate([dh, dh, dh, dm + h * six, dm + m * six, dl], axis=0)
    num = jnp.concatenate([nh, nh, nh, nm, nm, nl], axis=0)
    return jnp.concatenate([dist, num], axis=1).astype(jnp.bfloat16)


def source_features(stage, step, j, sub):
    h, m, l = split3(stage[pl.ds(j, 8, stride=step), :])
    hu = jnp.where(sub < 6, h, 1.0)
    mu = jnp.where(sub < 6, m, 1.0)
    return jnp.concatenate([h, m, l, hu, mu, hu], axis=0)


def phase_kernel(nb, chain, carry_in, carry_out, last, lists, *refs):
    own = not carry_in
    n = len(chain)
    n_msg = n - (1 if carry_in else 0)
    msgs, refs = refs[:n_msg], refs[n_msg:]
    if own:
        out, tgt, refs = refs[0], refs[1], refs[2:]
    else:
        before, tgt, src_in, out, refs = refs[0], refs[1], refs[2], refs[3], refs[4:]
    if carry_out:
        src_out, refs = refs[0], refs[1:]
    acc, stage, kept = refs[0], refs[1], list(refs[2:])
    src = ([src_in] if carry_in else []) + kept + ([src_out] if carry_out else [])
    width = 2 * nb + PAD
    sizes = [lists[7 * width + i] for i in chain]
    sub = lax.broadcasted_iota(jnp.int32, (8, BLK), 0)

    if own:
        acc[...] = jnp.zeros_like(acc)
        tgt[nb] = jnp.zeros((KF, 2 * BLK), jnp.bfloat16)
    else:
        acc[pl.ds(0, nb)] = before[...]

    step = nb // STEPS

    def make(k, i):
        msg = msgs[k - (1 if carry_in else 0)]
        for g in range(0, step, 8):
            rows = [msg[pl.ds(pl.multiple_of(c * nb + i * step + g, 8), 8), :] for c in range(6)]
            x, y, z, u, v, w = rows
            rows += [x * x + y * y + z * z, x * u + y * v + z * w]
            for c, value in enumerate(rows):
                stage[pl.ds(c * step + g, 8), :] = value
        for j in range(step):
            b = i * step + j
            f = source_features(stage, step, j, sub)
            src[k][pl.ds(pl.multiple_of(b * BLK, BLK), BLK), :KF] = f.astype(jnp.bfloat16).T
            if chain[k] == OWN:
                tgt[b] = target_features(msg, nb, b, sub)

    def tiles(slots, between):
        codes, prods = [], []
        for k, p in slots:
            codes.append(lists[chain[k] * width + p])
        for (k, _), code in zip(slots, codes):
            a = src[k][pl.ds(pl.multiple_of((code & 255) * BLK, BLK), BLK), :KF]
            prods.append(jnp.dot(a, tgt[code >> 12], preferred_element_type=jnp.float32))
        between()
        for code, p in zip(codes, prods):
            s = lax.rsqrt(p[:, :BLK])
            w = p[:, BLK:] * (s * (s * s))
            acc[code >> 12] += jnp.sum(w.reshape(16, 8, BLK), axis=0)

    if own:

        def first(i, _):
            make(0, i)
            return 0

        lax.fori_loop(0, STEPS, first, 0)

    for k in range(1, n):

        def both(i, _, k=k):
            tiles([(k - 1, i * U + u) for u in range(U)], lambda: make(k, i))
            return 0

        lax.fori_loop(0, STEPS, both, 0)

    groups = [([k for k in range(n - 1) if chain[k] != OWN or STEPS * U < nb], STEPS * U)]
    groups += [] if carry_out else [([n - 1], 0)]
    for group, done in groups:
        if not group:
            continue
        each = U // len(group)
        todo = jnp.int32(0)
        for k in group:
            todo = jnp.maximum(todo, (sizes[k] - done + each - 1) // each)

        def rest(i, _, group=group, each=each, done=done):
            at = done + i * each
            tiles([(k, jnp.minimum(at + u, width - 1)) for k in group for u in range(each)], lambda: None)
            return 0

        lax.fori_loop(0, todo, rest, 0)

    if last:

        def finish(i, _):
            out[pl.ds(pl.multiple_of(i * 8, 8), 8), :] = jnp.sum(acc[pl.ds(i * 8, 8)], axis=1)
            return 0

        lax.fori_loop(0, nb // 8, finish, 0, unroll=4)
    else:
        out[...] = acc[pl.ds(0, nb)]


def phase(name, chain, lists, msgs, before, carry_out):
    nb = msgs[0].shape[0] // 6
    carry_in = len(before) > 0
    last = not carry_out
    smem, vmem = pl.BlockSpec(memory_space=pltpu.SMEM), pl.BlockSpec(memory_space=pltpu.VMEM)
    args = [lists, *msgs, *before]
    shapes = [jax.ShapeDtypeStruct((nb, BLK) if last else (nb, 8, BLK), jnp.float32)]
    if not carry_in:
        shapes.append(jax.ShapeDtypeStruct((nb + 1, KF, 2 * BLK), jnp.bfloat16))
    if carry_out:
        shapes.append(jax.ShapeDtypeStruct((nb * BLK, BLK), jnp.bfloat16))
    kept = len(chain) - (1 if carry_in else 0) - (1 if carry_out else 0)
    return pl.pallas_call(
        functools.partial(phase_kernel, nb, tuple(chain), carry_in, carry_out, last),
        out_shape=shapes,
        in_specs=[smem] + [vmem] * (len(args) - 1),
        out_specs=[vmem] * len(shapes),
        scratch_shapes=[pltpu.VMEM((nb + 1, 8, BLK), jnp.float32), pltpu.VMEM((8 * nb // STEPS, BLK), jnp.float32)]
        + [pltpu.VMEM((nb * BLK, BLK), jnp.bfloat16)] * kept,
        compiler_params=pltpu.CompilerParams(vmem_limit_bytes=26 << 20),
        cost_estimate=pl.CostEstimate(
            flops=len(chain) * 2_000_000_000, bytes_accessed=len(chain) * 1_000_000, transcendentals=0
        ),
        name=name,
    )(*args)


def start_kernel(nb, rounds, *refs):
    outside, (msg, lists), inside, sems = refs[:5], refs[5:7], refs[7:12], refs[12]
    copies = [pltpu.make_async_copy(o, i, sems.at[n]) for n, (o, i) in enumerate(zip(outside, inside))]
    for copy in copies[::-1]:
        copy.start()
    pos, nrm, dens, index, count = inside

    def plane(i, _):
        for j in range(8):
            b = i * 8 + j
            at = pl.ds(pl.multiple_of(b * BLK, BLK), BLK)
            msg[pl.ds(b, 3, stride=nb), :] = pos[:, at]
            q = dens[pl.ds(b, 1), :] * (1.0 / (4.0 * math.pi))
            msg[pl.ds(3 * nb + b, 3, stride=nb), :] = nrm[:, at] * q
        return 0

    copies[4].wait()
    copies[3].wait()
    width = 2 * nb + PAD
    slots = index.shape[1]
    c = count[...]
    t_row = lax.broadcasted_iota(jnp.int32, (nb, nb), 0)
    t_col = lax.broadcasted_iota(jnp.int32, (nb, nb), 1)
    earlier = jnp.where(t_row < t_col, 1.0, 0.0).astype(jnp.bfloat16)
    pad = jnp.zeros((16 - rounds, nb), jnp.float32)
    cf = jnp.concatenate([c.astype(jnp.float32), pad], axis=0)
    before = jnp.dot(cf.astype(jnp.bfloat16), earlier, preferred_element_type=jnp.float32)
    size = jnp.sum(cf, axis=1, keepdims=True)
    place = lax.broadcasted_iota(jnp.int32, (1, width), 1)
    spot = lax.broadcasted_iota(jnp.int32, (width, nb), 0).astype(jnp.float32)
    t = lax.broadcasted_iota(jnp.int32, (1, nb), 1).astype(jnp.float32)
    rest = jnp.zeros((14, nb), jnp.float32)
    rows = []
    for r in range(rounds):
        both = jnp.zeros((16, width), jnp.float32)
        for s in range(slots):
            at = jnp.where(cf[r:r + 1] > s, before[r:r + 1] + s, -1.0)
            hot = jnp.where(spot == at, 1.0, 0.0).astype(jnp.bfloat16)
            code = jnp.concatenate([index[r, pl.ds(s, 1), :].astype(jnp.float32), t, rest], axis=0)
            both += lax.dot_general(
                code.astype(jnp.bfloat16), hot, (((1,), (1,)), ((), ())), preferred_element_type=jnp.float32
            )
        row = (both[1:2] * 4096.0 + both[0:1]).astype(jnp.int32)
        rows.append(jnp.where(place.astype(jnp.float32) < size[r:r + 1], row, nb << 12))
    rows.append(jnp.where(place < nb, (place << 12) + place, nb << 12))
    sub = lax.broadcasted_iota(jnp.int32, (16, BLK), 0)
    lane = lax.broadcasted_iota(jnp.int32, (16, BLK), 1)
    sizes = jnp.sum(jnp.where(sub == lane, size, 0.0), axis=0, keepdims=True)
    sizes = jnp.where(lane[:1] == rounds, float(nb), sizes).astype(jnp.int32)
    parts = width // BLK
    for i, row in enumerate(rows):
        for q in range(parts):
            lists[pl.ds(i * parts + q, 1), :] = row[:, q * BLK:(q + 1) * BLK]
    lists[pl.ds(len(rows) * parts, 1), :] = sizes
    for copy in copies[:3]:
        copy.wait()
    lax.fori_loop(0, nb // 8, plane, 0)


def start(positions, normals, strength, near_index, near_count):
    nb, rounds, slots = near_index.shape
    rows = (rounds + 2) * (slots * nb + PAD) // BLK
    vmem = pl.BlockSpec(memory_space=pltpu.VMEM)
    index = near_index.transpose(1, 2, 0)
    args = [positions, normals, strength.reshape(nb, BLK), index, near_count.T]
    msg, lists = pl.pallas_call(
        functools.partial(start_kernel, nb, rounds),
        out_shape=[
            jax.ShapeDtypeStruct((6 * nb, BLK), jnp.float32),
            jax.ShapeDtypeStruct((rows, BLK), jnp.int32),
        ],
        in_specs=[pl.BlockSpec(memory_space=pltpu.HBM)] * 5,
        out_specs=[vmem] * 2,
        scratch_shapes=[pltpu.VMEM(a.shape, a.dtype) for a in args] + [pltpu.SemaphoreType.DMA((5,))],
        compiler_params=pltpu.CompilerParams(vmem_limit_bytes=24 << 20),
        name="start",
    )(*[pltpu.with_memory_space_constraint(a, pltpu.HBM) for a in args])
    return msg, lists.reshape(-1)


def shards(positions, normals, strength, near_index, near_count):
    mine, lists = start(positions, normals, strength, near_index, near_count)
    top_bit = lax.axis_size("bulk").bit_length() - 2
    plan = [("grp", 0), ("grp", 1), ("bulk", 0), ("bulk", 1), ("bulk", 2), ("bulk", top_bit)]
    far = [from_partner(mine, axis, bit) for axis, bit in plan]
    a, tgt, held = phase("own_core", [OWN, 0], lists, [mine, far[0]], [], True)
    b, held = phase("mid", [0, 5, 1, 2], lists, [far[5], far[1], far[2]], [a, tgt, held], True)
    (c,) = phase("end", [2, 3, 4], lists, [far[3], far[4]], [b, tgt, held], False)
    return c.reshape(-1)


def solution(mesh):
    in_specs = (
        P(None, ("bulk", "grp")),
        P(None, ("bulk", "grp")),
        P(("bulk", "grp")),
        P(("bulk", "grp"), None, None),
        P(("bulk", "grp"), None),
    )
    out_specs = P(("bulk", "grp"))
    return jax.shard_map(shards, mesh=mesh, in_specs=in_specs, out_specs=out_specs, check_vma=False)
```

```python
import functools
import math

import jax
import jax.numpy as jnp
from jax import lax
from jax.experimental import pallas as pl
from jax.experimental.pallas import tpu as pltpu
from jax.sharding import PartitionSpec as P

DELTA2 = 0.05
BLK = 128
U = 52
KF = 48
STEPS = 4
PAD = 128
OWN = 6


def from_partner(x, axis, stride):
    return lax.ppermute(x, axis, [(i, i ^ 1 << stride) for i in range(lax.axis_size(axis))])


def split3(v):
    h = v.astype(jnp.bfloat16).astype(jnp.float32)
    r = v - h
    m = r.astype(jnp.bfloat16).astype(jnp.float32)
    return h, m, r - m


def row(msg, c, nb, b):
    return jnp.broadcast_to(msg[pl.ds(c * nb + b, 1), :], (8, BLK))


def target_features(msg, nb, b, sub):
    x, y, z = row(msg, 0, nb, b), row(msg, 1, nb, b), row(msg, 2, nb, b)
    k = jnp.where(sub < 3, sub, sub - 3)
    v = jnp.where(k == 0, x, jnp.where(k == 1, y, z))
    h, m, l = split3(jnp.where(sub < 6, v, x * x + y * y + z * z + DELTA2))
    for_dist = jnp.where(sub < 3, -2.0, 0.0)
    six = jnp.where(sub == 6, 1.0, 0.0)
    seven = jnp.where(sub == 7, -1.0, 0.0)
    is_six, mid = sub == 6, (sub >= 3) & (sub < 6)
    h2, m2 = h * for_dist, m * for_dist
    dh = h2 + six
    dmh, dmm = jnp.where(is_six, h, m2), jnp.where(is_six, m, m2)
    dl = l * (for_dist + six)
    nh, nm, nl = jnp.where(mid, h, seven), jnp.where(mid, m, 0.0), jnp.where(mid, l, 0.0)
    dist = jnp.concatenate([dh, dh, dh, dmh, dmm, dl], axis=0)
    num = jnp.concatenate([nh, nh, nh, nm, nm, nl], axis=0)
    return jnp.concatenate([dist, num], axis=1).astype(jnp.bfloat16)


def source_features(stage, step, j, sub):
    h, m, l = split3(stage[pl.ds(j, 8, stride=step), :])
    hu = jnp.where(sub < 6, h, 1.0)
    mu = jnp.where(sub < 6, m, 1.0)
    return jnp.concatenate([h, m, l, hu, mu, hu], axis=0)


def phase_kernel(nb, chain, carry_in, carry_out, last, lists, *refs):
    own = not carry_in
    n = len(chain)
    n_msg = n - (1 if carry_in else 0)
    msgs, refs = refs[:n_msg], refs[n_msg:]
    if own:
        out, tgt, refs = refs[0], refs[1], refs[2:]
    else:
        before, tgt, src_in, out, refs = refs[0], refs[1], refs[2], refs[3], refs[4:]
    if carry_out:
        src_out, refs = refs[0], refs[1:]
    acc, stage, kept = refs[0], refs[1], list(refs[2:])
    src = ([src_in] if carry_in else []) + kept + ([src_out] if carry_out else [])
    width = 2 * nb + PAD
    sizes = [lists[7 * width + i] for i in chain]
    sub = lax.broadcasted_iota(jnp.int32, (8, BLK), 0)

    if own:
        acc[...] = jnp.zeros_like(acc)
        tgt[nb] = jnp.zeros((KF, 2 * BLK), jnp.bfloat16)
    else:
        acc[pl.ds(0, nb)] = before[...]

    step = nb // STEPS

    def make(k, i):
        msg = msgs[k - (1 if carry_in else 0)]
        for g in range(0, step, 8):
            rows = [msg[pl.ds(pl.multiple_of(c * nb + i * step + g, 8), 8), :] for c in range(6)]
            x, y, z, u, v, w = rows
            rows += [x * x + y * y + z * z, x * u + y * v + z * w]
            for c, value in enumerate(rows):
                stage[pl.ds(c * step + g, 8), :] = value
        for j in range(step):
            b = i * step + j
            f = source_features(stage, step, j, sub)
            src[k][pl.ds(pl.multiple_of(b * BLK, BLK), BLK), :KF] = f.astype(jnp.bfloat16).T
            if chain[k] == OWN:
                tgt[b] = target_features(msg, nb, b, sub)

    def tiles(slots, between):
        codes, prods = [], []
        for k, p in slots:
            codes.append(lists[chain[k] * width + p])
        for (k, _), code in zip(slots, codes):
            a = src[k][pl.ds(pl.multiple_of((code & 255) * BLK, BLK), BLK), :KF]
            prods.append(jnp.dot(a, tgt[code >> 12], preferred_element_type=jnp.float32))
        between()
        for code, p in zip(codes, prods):
            s = lax.rsqrt(p[:, :BLK])
            w = p[:, BLK:] * (s * (s * s))
            acc[code >> 12] += jnp.sum(w.reshape(16, 8, BLK), axis=0)

    if own:

        def first(i, _):
            make(0, i)
            return 0

        lax.fori_loop(0, STEPS, first, 0)

    for k in range(1, n):

        def both(i, _, k=k):
            each = step if chain[k - 1] == OWN else U
            tiles([(k - 1, i * each + u) for u in range(each)], lambda: make(k, i))
            return 0

        lax.fori_loop(0, STEPS, both, 0)

    groups = [([k for k in range(n - 1) if chain[k] != OWN], STEPS * U)]
    groups += [] if carry_out else [([n - 1], 0)]
    for group, done in groups:
        if not group:
            continue
        each = U // len(group)
        todo = jnp.int32(0)
        for k in group:
            todo = jnp.maximum(todo, (sizes[k] - done + each - 1) // each)

        def rest(i, _, group=group, each=each, done=done):
            at = done + i * each
            tiles([(k, jnp.minimum(at + u, width - 1)) for k in group for u in range(each)], lambda: None)
            return 0

        lax.fori_loop(0, todo, rest, 0)

    if last:

        def finish(i, _):
            out[pl.ds(pl.multiple_of(i * 8, 8), 8), :] = jnp.sum(acc[pl.ds(i * 8, 8)], axis=1)
            return 0

        lax.fori_loop(0, nb // 8, finish, 0, unroll=4)
    else:
        out[...] = acc[pl.ds(0, nb)]


def phase(name, chain, lists, msgs, before, carry_out):
    nb = msgs[0].shape[0] // 6
    carry_in = len(before) > 0
    last = not carry_out
    smem, vmem = pl.BlockSpec(memory_space=pltpu.SMEM), pl.BlockSpec(memory_space=pltpu.VMEM)
    args = [lists, *msgs, *before]
    shapes = [jax.ShapeDtypeStruct((nb, BLK) if last else (nb, 8, BLK), jnp.float32)]
    if not carry_in:
        shapes.append(jax.ShapeDtypeStruct((nb + 1, KF, 2 * BLK), jnp.bfloat16))
    if carry_out:
        shapes.append(jax.ShapeDtypeStruct((nb * BLK, BLK), jnp.bfloat16))
    kept = len(chain) - (1 if carry_in else 0) - (1 if carry_out else 0)
    return pl.pallas_call(
        functools.partial(phase_kernel, nb, tuple(chain), carry_in, carry_out, last),
        out_shape=shapes,
        in_specs=[smem] + [vmem] * (len(args) - 1),
        out_specs=[vmem] * len(shapes),
        scratch_shapes=[pltpu.VMEM((nb + 1, 8, BLK), jnp.float32), pltpu.VMEM((8 * nb // STEPS, BLK), jnp.float32)]
        + [pltpu.VMEM((nb * BLK, BLK), jnp.bfloat16)] * kept,
        compiler_params=pltpu.CompilerParams(vmem_limit_bytes=26 << 20),
        cost_estimate=pl.CostEstimate(
            flops=len(chain) * 2_000_000_000, bytes_accessed=len(chain) * 1_000_000, transcendentals=0
        ),
        name=name,
    )(*args)


def start_kernel(nb, rounds, *refs):
    outside, (msg, lists), inside, sems = refs[:5], refs[5:7], refs[7:12], refs[12]
    copies = [pltpu.make_async_copy(o, i, sems.at[n]) for n, (o, i) in enumerate(zip(outside, inside))]
    for copy in copies[::-1]:
        copy.start()
    pos, nrm, dens, index, count = inside

    def plane(i, _):
        for j in range(8):
            b = i * 8 + j
            at = pl.ds(pl.multiple_of(b * BLK, BLK), BLK)
            msg[pl.ds(b, 3, stride=nb), :] = pos[:, at]
            q = dens[pl.ds(b, 1), :] * (1.0 / (4.0 * math.pi))
            msg[pl.ds(3 * nb + b, 3, stride=nb), :] = nrm[:, at] * q
        return 0

    copies[4].wait()
    copies[3].wait()
    width = 2 * nb + PAD
    slots = index.shape[1]
    c = count[...]
    t_row = lax.broadcasted_iota(jnp.int32, (nb, nb), 0)
    t_col = lax.broadcasted_iota(jnp.int32, (nb, nb), 1)
    earlier = jnp.where(t_row < t_col, 1.0, 0.0).astype(jnp.bfloat16)
    pad = jnp.zeros((16 - rounds, nb), jnp.float32)
    cf = jnp.concatenate([c.astype(jnp.float32), pad], axis=0)
    before = jnp.dot(cf.astype(jnp.bfloat16), earlier, preferred_element_type=jnp.float32)
    size = jnp.sum(cf, axis=1, keepdims=True)
    place = lax.broadcasted_iota(jnp.int32, (1, width), 1)
    spot = lax.broadcasted_iota(jnp.int32, (width, nb), 0).astype(jnp.float32)
    t = lax.broadcasted_iota(jnp.int32, (1, nb), 1).astype(jnp.float32)
    rest = jnp.zeros((14, nb), jnp.float32)
    rows = []
    for r in range(rounds):
        both = jnp.zeros((16, width), jnp.float32)
        for s in range(slots):
            at = jnp.where(cf[r:r + 1] > s, before[r:r + 1] + s, -1.0)
            hot = jnp.where(spot == at, 1.0, 0.0).astype(jnp.bfloat16)
            code = jnp.concatenate([index[r, pl.ds(s, 1), :].astype(jnp.float32), t, rest], axis=0)
            both += lax.dot_general(
                code.astype(jnp.bfloat16), hot, (((1,), (1,)), ((), ())), preferred_element_type=jnp.float32
            )
        row = (both[1:2] * 4096.0 + both[0:1]).astype(jnp.int32)
        rows.append(jnp.where(place.astype(jnp.float32) < size[r:r + 1], row, nb << 12))
    rows.append(jnp.where(place < nb, (place << 12) + place, nb << 12))
    sub = lax.broadcasted_iota(jnp.int32, (16, BLK), 0)
    lane = lax.broadcasted_iota(jnp.int32, (16, BLK), 1)
    sizes = jnp.sum(jnp.where(sub == lane, size, 0.0), axis=0, keepdims=True)
    sizes = jnp.where(lane[:1] == rounds, float(nb), sizes).astype(jnp.int32)
    parts = width // BLK
    for i, row in enumerate(rows):
        for q in range(parts):
            lists[pl.ds(i * parts + q, 1), :] = row[:, q * BLK:(q + 1) * BLK]
    lists[pl.ds(len(rows) * parts, 1), :] = sizes
    for copy in copies[:3]:
        copy.wait()
    lax.fori_loop(0, nb // 8, plane, 0)


def start(positions, normals, strength, near_index, near_count):
    nb, rounds, slots = near_index.shape
    rows = (rounds + 2) * (slots * nb + PAD) // BLK
    vmem = pl.BlockSpec(memory_space=pltpu.VMEM)
    index = near_index.transpose(1, 2, 0)
    args = [positions, normals, strength.reshape(nb, BLK), index, near_count.T]
    msg, lists = pl.pallas_call(
        functools.partial(start_kernel, nb, rounds),
        out_shape=[
            jax.ShapeDtypeStruct((6 * nb, BLK), jnp.float32),
            jax.ShapeDtypeStruct((rows, BLK), jnp.int32),
        ],
        in_specs=[pl.BlockSpec(memory_space=pltpu.HBM)] * 5,
        out_specs=[vmem] * 2,
        scratch_shapes=[pltpu.VMEM(a.shape, a.dtype) for a in args] + [pltpu.SemaphoreType.DMA((5,))],
        compiler_params=pltpu.CompilerParams(vmem_limit_bytes=24 << 20),
        name="start",
    )(*[pltpu.with_memory_space_constraint(a, pltpu.HBM) for a in args])
    return msg, lists.reshape(-1)


def shards(positions, normals, strength, near_index, near_count):
    mine, lists = start(positions, normals, strength, near_index, near_count)
    top_bit = lax.axis_size("bulk").bit_length() - 2
    plan = [("grp", 0), ("grp", 1), ("bulk", 0), ("bulk", 1), ("bulk", 2), ("bulk", top_bit)]
    far = [from_partner(mine, axis, bit) for axis, bit in plan]
    a, tgt, held = phase("own_core", [OWN, 0], lists, [mine, far[0]], [], True)
    b, held = phase("mid", [0, 2, 1, 5], lists, [far[2], far[1], far[5]], [a, tgt, held], True)
    (c,) = phase("end", [5, 3, 4], lists, [far[3], far[4]], [b, tgt, held], False)
    return c.reshape(-1)


def solution(mesh):
    in_specs = (
        P(None, ("bulk", "grp")),
        P(None, ("bulk", "grp")),
        P(("bulk", "grp")),
        P(("bulk", "grp"), None, None),
        P(("bulk", "grp"), None),
    )
    out_specs = P(("bulk", "grp"))
    return jax.shard_map(shards, mesh=mesh, in_specs=in_specs, out_specs=out_specs, check_vma=False)
```

```python
import functools
import math

import jax
import jax.numpy as jnp
from jax import lax
from jax.experimental import pallas as pl
from jax.experimental.pallas import tpu as pltpu
from jax.sharding import PartitionSpec as P

DELTA2 = 0.05
BLK = 128
U = 52
KF = 48
STEPS = 4
PAD = 128
OWN = 6


def from_partner(x, axis, stride):
    return lax.ppermute(x, axis, [(i, i ^ 1 << stride) for i in range(lax.axis_size(axis))])


def split3(v):
    h = v.astype(jnp.bfloat16).astype(jnp.float32)
    r = v - h
    m = r.astype(jnp.bfloat16).astype(jnp.float32)
    return h, m, r - m


def row(msg, c, nb, b):
    return jnp.broadcast_to(msg[pl.ds(c * nb + b, 1), :], (8, BLK))


def target_features(msg, nb, b, sub):
    x, y, z = row(msg, 0, nb, b), row(msg, 1, nb, b), row(msg, 2, nb, b)
    k = jnp.where(sub < 3, sub, sub - 3)
    v = jnp.where(k == 0, x, jnp.where(k == 1, y, z))
    h, m, l = split3(jnp.where(sub < 6, v, x * x + y * y + z * z + DELTA2))
    for_dist = jnp.where(sub < 3, -2.0, 0.0)
    six = jnp.where(sub == 6, 1.0, 0.0)
    seven = jnp.where(sub == 7, -1.0, 0.0)
    is_six, mid = sub == 6, (sub >= 3) & (sub < 6)
    h2, m2 = h * for_dist, m * for_dist
    dh = h2 + six
    dmh, dmm = jnp.where(is_six, h, m2), jnp.where(is_six, m, m2)
    dl = l * (for_dist + six)
    nh, nm, nl = jnp.where(mid, h, seven), jnp.where(mid, m, 0.0), jnp.where(mid, l, 0.0)
    dist = jnp.concatenate([dh, dh, dh, dmh, dmm, dl], axis=0)
    num = jnp.concatenate([nh, nh, nh, nm, nm, nl], axis=0)
    return jnp.concatenate([dist, num], axis=1).astype(jnp.bfloat16)


def source_features(stage, step, j, sub):
    h, m, l = split3(stage[pl.ds(j, 8, stride=step), :])
    hu = jnp.where(sub < 6, h, 1.0)
    mu = jnp.where(sub < 6, m, 1.0)
    return jnp.concatenate([h, m, l, hu, mu, hu], axis=0)


def phase_kernel(nb, chain, carry_in, carry_out, last, lists_in, *refs):
    own = not carry_in
    n = len(chain)
    n_msg = n - (1 if carry_in else 0)
    msgs, refs = refs[:n_msg], refs[n_msg:]
    if own:
        out, tgt, refs = refs[0], refs[1], refs[2:]
    else:
        before, tgt, src_in, out, refs = refs[0], refs[1], refs[2], refs[3], refs[4:]
    if carry_out:
        src_out, refs = refs[0], refs[1:]
    acc, stage, lists, sem, kept = refs[0], refs[1], refs[2], refs[3], list(refs[4:])
    copy = pltpu.make_async_copy(lists_in, lists, sem)
    copy.start()
    src = ([src_in] if carry_in else []) + kept + ([src_out] if carry_out else [])
    width = 2 * nb + PAD
    sub = lax.broadcasted_iota(jnp.int32, (8, BLK), 0)

    if own:
        acc[...] = jnp.zeros_like(acc)
        tgt[nb] = jnp.zeros((KF, 2 * BLK), jnp.bfloat16)
    else:
        acc[pl.ds(0, nb)] = before[...]

    step = nb // STEPS

    def make(k, i):
        msg = msgs[k - (1 if carry_in else 0)]
        for g in range(0, step, 8):
            rows = [msg[pl.ds(pl.multiple_of(c * nb + i * step + g, 8), 8), :] for c in range(6)]
            x, y, z, u, v, w = rows
            rows += [x * x + y * y + z * z, x * u + y * v + z * w]
            for c, value in enumerate(rows):
                stage[pl.ds(c * step + g, 8), :] = value
        for j in range(step):
            b = i * step + j
            f = source_features(stage, step, j, sub)
            src[k][pl.ds(pl.multiple_of(b * BLK, BLK), BLK), :KF] = f.astype(jnp.bfloat16).T
            if chain[k] == OWN:
                tgt[b] = target_features(msg, nb, b, sub)

    def tiles(slots, between):
        codes, prods = [], []
        for k, p in slots:
            codes.append(lists[chain[k] * width + p])
        for (k, _), code in zip(slots, codes):
            a = src[k][pl.ds(pl.multiple_of((code & 255) * BLK, BLK), BLK), :KF]
            prods.append(jnp.dot(a, tgt[code >> 12], preferred_element_type=jnp.float32))
        between()
        for code, p in zip(codes, prods):
            s = lax.rsqrt(p[:, :BLK])
            w = p[:, BLK:] * (s * (s * s))
            acc[code >> 12] += jnp.sum(w.reshape(16, 8, BLK), axis=0)

    if own:

        def first(i, _):
            make(0, i)
            return 0

        lax.fori_loop(0, STEPS, first, 0)

    copy.wait()
    sizes = [lists[7 * width + i] for i in chain]
    for k in range(1, n):

        def both(i, _, k=k):
            each = step if chain[k - 1] == OWN else U
            tiles([(k - 1, i * each + u) for u in range(each)], lambda: make(k, i))
            return 0

        lax.fori_loop(0, STEPS, both, 0)

    groups = [([k for k in range(n - 1) if chain[k] != OWN], STEPS * U)]
    groups += [] if carry_out else [([n - 1], 0)]
    for group, done in groups:
        if not group:
            continue
        each = U // len(group)
        todo = jnp.int32(0)
        for k in group:
            todo = jnp.maximum(todo, (sizes[k] - done + each - 1) // each)

        def rest(i, _, group=group, each=each, done=done):
            at = done + i * each
            tiles([(k, jnp.minimum(at + u, width - 1)) for k in group for u in range(each)], lambda: None)
            return 0

        lax.fori_loop(0, todo, rest, 0)

    if last:

        def finish(i, _):
            out[pl.ds(pl.multiple_of(i * 8, 8), 8), :] = jnp.sum(acc[pl.ds(i * 8, 8)], axis=1)
            return 0

        lax.fori_loop(0, nb // 8, finish, 0, unroll=4)
    else:
        out[...] = acc[pl.ds(0, nb)]


def phase(name, chain, lists, msgs, before, carry_out):
    nb = msgs[0].shape[0] // 6
    carry_in = len(before) > 0
    last = not carry_out
    near, vmem = pl.BlockSpec(memory_space=pl.ANY), pl.BlockSpec(memory_space=pltpu.VMEM)
    args = [lists, *msgs, *before]
    shapes = [jax.ShapeDtypeStruct((nb, BLK) if last else (nb, 8, BLK), jnp.float32)]
    if not carry_in:
        shapes.append(jax.ShapeDtypeStruct((nb + 1, KF, 2 * BLK), jnp.bfloat16))
    if carry_out:
        shapes.append(jax.ShapeDtypeStruct((nb * BLK, BLK), jnp.bfloat16))
    kept = len(chain) - (1 if carry_in else 0) - (1 if carry_out else 0)
    return pl.pallas_call(
        functools.partial(phase_kernel, nb, tuple(chain), carry_in, carry_out, last),
        out_shape=shapes,
        in_specs=[near] + [vmem] * (len(args) - 1),
        out_specs=[vmem] * len(shapes),
        scratch_shapes=[pltpu.VMEM((nb + 1, 8, BLK), jnp.float32), pltpu.VMEM((8 * nb // STEPS, BLK), jnp.float32)]
        + [pltpu.SMEM(lists.shape, jnp.int32), pltpu.SemaphoreType.DMA]
        + [pltpu.VMEM((nb * BLK, BLK), jnp.bfloat16)] * kept,
        compiler_params=pltpu.CompilerParams(vmem_limit_bytes=26 << 20),
        cost_estimate=pl.CostEstimate(
            flops=len(chain) * 2_000_000_000, bytes_accessed=len(chain) * 1_000_000, transcendentals=0
        ),
        name=name,
    )(*args)


def start_kernel(nb, rounds, *refs):
    outside, (msg, lists), inside, sems = refs[:5], refs[5:7], refs[7:12], refs[12]
    copies = [pltpu.make_async_copy(o, i, sems.at[n]) for n, (o, i) in enumerate(zip(outside, inside))]
    for copy in copies[::-1]:
        copy.start()
    pos, nrm, dens, index, count = inside

    def plane(i, _):
        for j in range(8):
            b = i * 8 + j
            at = pl.ds(pl.multiple_of(b * BLK, BLK), BLK)
            msg[pl.ds(b, 3, stride=nb), :] = pos[:, at]
            q = dens[pl.ds(b, 1), :] * (1.0 / (4.0 * math.pi))
            msg[pl.ds(3 * nb + b, 3, stride=nb), :] = nrm[:, at] * q
        return 0

    copies[4].wait()
    copies[3].wait()
    width = 2 * nb + PAD
    slots = index.shape[1]
    c = count[...]
    t_row = lax.broadcasted_iota(jnp.int32, (nb, nb), 0)
    t_col = lax.broadcasted_iota(jnp.int32, (nb, nb), 1)
    earlier = jnp.where(t_row < t_col, 1.0, 0.0).astype(jnp.bfloat16)
    pad = jnp.zeros((16 - rounds, nb), jnp.float32)
    cf = jnp.concatenate([c.astype(jnp.float32), pad], axis=0)
    before = jnp.dot(cf.astype(jnp.bfloat16), earlier, preferred_element_type=jnp.float32)
    size = jnp.sum(cf, axis=1, keepdims=True)
    place = lax.broadcasted_iota(jnp.int32, (1, width), 1)
    spot = lax.broadcasted_iota(jnp.int32, (width, nb), 0).astype(jnp.float32)
    t = lax.broadcasted_iota(jnp.int32, (1, nb), 1).astype(jnp.float32)
    rest = jnp.zeros((14, nb), jnp.float32)
    rows = []
    for r in range(rounds):
        both = jnp.zeros((16, width), jnp.float32)
        for s in range(slots):
            at = jnp.where(cf[r:r + 1] > s, before[r:r + 1] + s, -1.0)
            hot = jnp.where(spot == at, 1.0, 0.0).astype(jnp.bfloat16)
            code = jnp.concatenate([index[r, pl.ds(s, 1), :].astype(jnp.float32), t, rest], axis=0)
            both += lax.dot_general(
                code.astype(jnp.bfloat16), hot, (((1,), (1,)), ((), ())), preferred_element_type=jnp.float32
            )
        row = (both[1:2] * 4096.0 + both[0:1]).astype(jnp.int32)
        rows.append(jnp.where(place.astype(jnp.float32) < size[r:r + 1], row, nb << 12))
    rows.append(jnp.where(place < nb, (place << 12) + place, nb << 12))
    sub = lax.broadcasted_iota(jnp.int32, (16, BLK), 0)
    lane = lax.broadcasted_iota(jnp.int32, (16, BLK), 1)
    sizes = jnp.sum(jnp.where(sub == lane, size, 0.0), axis=0, keepdims=True)
    sizes = jnp.where(lane[:1] == rounds, float(nb), sizes).astype(jnp.int32)
    parts = width // BLK
    for i, row in enumerate(rows):
        for q in range(parts):
            lists[pl.ds(i * parts + q, 1), :] = row[:, q * BLK:(q + 1) * BLK]
    lists[pl.ds(len(rows) * parts, 1), :] = sizes
    for copy in copies[:3]:
        copy.wait()
    lax.fori_loop(0, nb // 8, plane, 0)


def start(positions, normals, strength, near_index, near_count):
    nb, rounds, slots = near_index.shape
    rows = (rounds + 2) * (slots * nb + PAD) // BLK
    vmem = pl.BlockSpec(memory_space=pltpu.VMEM)
    index = near_index.transpose(1, 2, 0)
    args = [positions, normals, strength.reshape(nb, BLK), index, near_count.T]
    msg, lists = pl.pallas_call(
        functools.partial(start_kernel, nb, rounds),
        out_shape=[
            jax.ShapeDtypeStruct((6 * nb, BLK), jnp.float32),
            jax.ShapeDtypeStruct((rows, BLK), jnp.int32),
        ],
        in_specs=[pl.BlockSpec(memory_space=pltpu.HBM)] * 5,
        out_specs=[vmem] * 2,
        scratch_shapes=[pltpu.VMEM(a.shape, a.dtype) for a in args] + [pltpu.SemaphoreType.DMA((5,))],
        compiler_params=pltpu.CompilerParams(vmem_limit_bytes=24 << 20),
        name="start",
    )(*[pltpu.with_memory_space_constraint(a, pltpu.HBM) for a in args])
    return msg, lists.reshape(-1)


def shards(positions, normals, strength, near_index, near_count):
    mine, lists = start(positions, normals, strength, near_index, near_count)
    top_bit = lax.axis_size("bulk").bit_length() - 2
    plan = [("grp", 0), ("grp", 1), ("bulk", 0), ("bulk", 1), ("bulk", 2), ("bulk", top_bit)]
    far = [from_partner(mine, axis, bit) for axis, bit in plan]
    a, tgt, held = phase("own_core", [OWN, 0], lists, [mine, far[0]], [], True)
    b, held = phase("mid", [0, 2, 1, 5], lists, [far[2], far[1], far[5]], [a, tgt, held], True)
    (c,) = phase("end", [5, 3, 4], lists, [far[3], far[4]], [b, tgt, held], False)
    return c.reshape(-1)


def solution(mesh):
    in_specs = (
        P(None, ("bulk", "grp")),
        P(None, ("bulk", "grp")),
        P(("bulk", "grp")),
        P(("bulk", "grp"), None, None),
        P(("bulk", "grp"), None),
    )
    out_specs = P(("bulk", "grp"))
    return jax.shard_map(shards, mesh=mesh, in_specs=in_specs, out_specs=out_specs, check_vma=False)
```

```python
import functools
import math

import jax
import jax.numpy as jnp
from jax import lax
from jax.experimental import pallas as pl
from jax.experimental.pallas import tpu as pltpu
from jax.sharding import PartitionSpec as P

DELTA2 = 0.05
BLK = 128
U = 52
KF = 48
STEPS = 4
PAD = 128
OWN = 6


def from_partner(x, axis, stride):
    return lax.ppermute(x, axis, [(i, i ^ 1 << stride) for i in range(lax.axis_size(axis))])


def split3(v):
    h = v.astype(jnp.bfloat16).astype(jnp.float32)
    r = v - h
    m = r.astype(jnp.bfloat16).astype(jnp.float32)
    return h, m, r - m


def row(msg, c, nb, b):
    return jnp.broadcast_to(msg[pl.ds(c * nb + b, 1), :], (8, BLK))


def target_features(msg, nb, b, sub):
    x, y, z = row(msg, 0, nb, b), row(msg, 1, nb, b), row(msg, 2, nb, b)
    k = jnp.where(sub < 3, sub, sub - 3)
    v = jnp.where(k == 0, x, jnp.where(k == 1, y, z))
    h, m, l = split3(jnp.where(sub < 6, v, x * x + y * y + z * z + DELTA2))
    for_dist = jnp.where(sub < 3, -2.0, 0.0)
    six = jnp.where(sub == 6, 1.0, 0.0)
    seven = jnp.where(sub == 7, -1.0, 0.0)
    is_six, mid = sub == 6, (sub >= 3) & (sub < 6)
    h2, m2 = h * for_dist, m * for_dist
    dh = h2 + six
    dmh, dmm = jnp.where(is_six, h, m2), jnp.where(is_six, m, m2)
    dl = l * (for_dist + six)
    nh, nm, nl = jnp.where(mid, h, seven), jnp.where(mid, m, 0.0), jnp.where(mid, l, 0.0)
    dist = jnp.concatenate([dh, dh, dh, dmh, dmm, dl], axis=0)
    num = jnp.concatenate([nh, nh, nh, nm, nm, nl], axis=0)
    return jnp.concatenate([dist, num], axis=1).astype(jnp.bfloat16)


def source_features(stage, step, j, sub):
    h, m, l = split3(stage[pl.ds(j, 8, stride=step), :])
    hu = jnp.where(sub < 6, h, 1.0)
    mu = jnp.where(sub < 6, m, 1.0)
    return jnp.concatenate([h, m, l, hu, mu, hu], axis=0)


def phase_kernel(nb, chain, carry_in, carry_out, last, lists_in, *refs):
    own = not carry_in
    n = len(chain)
    n_msg = n - (1 if carry_in else 0)
    msgs, refs = refs[:n_msg], refs[n_msg:]
    if own:
        out, tgt, refs = refs[0], refs[1], refs[2:]
    else:
        before, tgt, src_in, out, refs = refs[0], refs[1], refs[2], refs[3], refs[4:]
    if carry_out:
        src_out, refs = refs[0], refs[1:]
    acc, stage, lists, sem, kept = refs[0], refs[1], refs[2], refs[3], list(refs[4:])
    copy = pltpu.make_async_copy(lists_in, lists, sem)
    copy.start()
    src = ([src_in] if carry_in else []) + kept + ([src_out] if carry_out else [])
    width = 2 * nb + PAD
    sub = lax.broadcasted_iota(jnp.int32, (8, BLK), 0)

    if own:
        acc[...] = jnp.zeros_like(acc)
        tgt[nb] = jnp.zeros((KF, 2 * BLK), jnp.bfloat16)
    else:
        acc[pl.ds(0, nb)] = before[...]

    step = nb // STEPS

    def make(k, i):
        msg = msgs[k - (1 if carry_in else 0)]
        for g in range(0, step, 8):
            rows = [msg[pl.ds(pl.multiple_of(c * nb + i * step + g, 8), 8), :] for c in range(6)]
            x, y, z, u, v, w = rows
            rows += [x * x + y * y + z * z, x * u + y * v + z * w]
            for c, value in enumerate(rows):
                stage[pl.ds(c * step + g, 8), :] = value
        for j in range(step):
            b = i * step + j
            f = source_features(stage, step, j, sub)
            src[k][pl.ds(pl.multiple_of(b * BLK, BLK), BLK), :KF] = f.astype(jnp.bfloat16).T
            if chain[k] == OWN:
                tgt[b] = target_features(msg, nb, b, sub)

    def tiles(slots, between):
        codes, prods = [], []
        for k, p in slots:
            codes.append(lists[chain[k] * width + p])
        for (k, _), code in zip(slots, codes):
            a = src[k][pl.ds(pl.multiple_of((code & 255) * BLK, BLK), BLK), :KF]
            prods.append(jnp.dot(a, tgt[code >> 12], preferred_element_type=jnp.float32))
        between()
        for code, p in zip(codes, prods):
            s = lax.rsqrt(p[:, :BLK])
            w = p[:, BLK:] * (s * (s * s))
            acc[code >> 12] += jnp.sum(w.reshape(16, 8, BLK), axis=0)

    if own:

        def first(i, _):
            make(0, i)
            return 0

        lax.fori_loop(0, STEPS, first, 0)

    copy.wait()
    sizes = [lists[7 * width + i] for i in chain]
    for k in range(1, n):

        def both(i, _, k=k):
            each = step if chain[k - 1] == OWN else U
            tiles([(k - 1, i * each + u) for u in range(each)], lambda: make(k, i))
            return 0

        lax.fori_loop(0, STEPS, both, 0)

    groups = [([k for k in range(n - 1) if chain[k] != OWN], STEPS * U)]
    groups += [] if carry_out else [([n - 1], 0)]
    for group, done in groups:
        if not group:
            continue
        each = U // len(group)
        todo = jnp.int32(0)
        for k in group:
            todo = jnp.maximum(todo, (sizes[k] - done + each - 1) // each)

        def rest(i, _, group=group, each=each, done=done):
            at = done + i * each
            tiles([(k, jnp.minimum(at + u, width - 1)) for k in group for u in range(each)], lambda: None)
            return 0

        lax.fori_loop(0, todo, rest, 0)

    if last:

        def finish(i, _):
            out[pl.ds(pl.multiple_of(i * 8, 8), 8), :] = jnp.sum(acc[pl.ds(i * 8, 8)], axis=1)
            return 0

        lax.fori_loop(0, nb // 8, finish, 0, unroll=4)
    else:
        out[...] = acc[pl.ds(0, nb)]


def phase(name, chain, lists, msgs, before, carry_out):
    nb = msgs[0].shape[0] // 6
    carry_in = len(before) > 0
    last = not carry_out
    near, vmem = pl.BlockSpec(memory_space=pl.ANY), pl.BlockSpec(memory_space=pltpu.VMEM)
    args = [lists, *msgs, *before]
    shapes = [jax.ShapeDtypeStruct((nb, BLK) if last else (nb, 8, BLK), jnp.float32)]
    if not carry_in:
        shapes.append(jax.ShapeDtypeStruct((nb + 1, KF, 2 * BLK), jnp.bfloat16))
    if carry_out:
        shapes.append(jax.ShapeDtypeStruct((nb * BLK, BLK), jnp.bfloat16))
    kept = len(chain) - (1 if carry_in else 0) - (1 if carry_out else 0)
    return pl.pallas_call(
        functools.partial(phase_kernel, nb, tuple(chain), carry_in, carry_out, last),
        out_shape=shapes,
        in_specs=[near] + [vmem] * (len(args) - 1),
        out_specs=[vmem] * len(shapes),
        scratch_shapes=[pltpu.VMEM((nb + 1, 8, BLK), jnp.float32), pltpu.VMEM((8 * nb // STEPS, BLK), jnp.float32)]
        + [pltpu.SMEM(lists.shape, jnp.int32), pltpu.SemaphoreType.DMA]
        + [pltpu.VMEM((nb * BLK, BLK), jnp.bfloat16)] * kept,
        compiler_params=pltpu.CompilerParams(vmem_limit_bytes=26 << 20),
        cost_estimate=pl.CostEstimate(
            flops=len(chain) * 2_000_000_000, bytes_accessed=len(chain) * 1_000_000, transcendentals=0
        ),
        name=name,
    )(*args)


def start_kernel(nb, rounds, *refs):
    outside, (msg, lists), inside, sems = refs[:5], refs[5:7], refs[7:12], refs[12]
    copies = [pltpu.make_async_copy(o, i, sems.at[n]) for n, (o, i) in enumerate(zip(outside, inside))]
    for copy in copies[::-1]:
        copy.start()
    pos, nrm, dens, index, count = inside

    def plane(i, _):
        for j in range(8):
            b = i * 8 + j
            at = pl.ds(pl.multiple_of(b * BLK, BLK), BLK)
            msg[pl.ds(b, 3, stride=nb), :] = pos[:, at]
            q = dens[pl.ds(b, 1), :] * (1.0 / (4.0 * math.pi))
            msg[pl.ds(3 * nb + b, 3, stride=nb), :] = nrm[:, at] * q
        return 0

    copies[4].wait()
    copies[3].wait()
    width = 2 * nb + PAD
    slots = index.shape[1]
    c = count[...]
    t_row = lax.broadcasted_iota(jnp.int32, (nb, nb), 0)
    t_col = lax.broadcasted_iota(jnp.int32, (nb, nb), 1)
    earlier = jnp.where(t_row < t_col, 1.0, 0.0).astype(jnp.bfloat16)
    pad = jnp.zeros((16 - rounds, nb), jnp.float32)
    cf = jnp.concatenate([c.astype(jnp.float32), pad], axis=0)
    before = jnp.dot(cf.astype(jnp.bfloat16), earlier, preferred_element_type=jnp.float32)
    size = jnp.sum(cf, axis=1, keepdims=True)
    place = lax.broadcasted_iota(jnp.int32, (1, width), 1)
    spot = lax.broadcasted_iota(jnp.int32, (width, nb), 0).astype(jnp.float32)
    t = lax.broadcasted_iota(jnp.int32, (1, nb), 1).astype(jnp.float32)
    rest = jnp.zeros((14, nb), jnp.float32)
    rows = []
    for r in range(rounds):
        both = jnp.zeros((16, width), jnp.float32)
        for s in range(slots):
            at = jnp.where(cf[r:r + 1] > s, before[r:r + 1] + s, -1.0)
            hot = jnp.where(spot == at, 1.0, 0.0).astype(jnp.bfloat16)
            code = jnp.concatenate([index[r, pl.ds(s, 1), :].astype(jnp.float32), t, rest], axis=0)
            both += lax.dot_general(
                code.astype(jnp.bfloat16), hot, (((1,), (1,)), ((), ())), preferred_element_type=jnp.float32
            )
        row = (both[1:2] * 4096.0 + both[0:1]).astype(jnp.int32)
        rows.append(jnp.where(place.astype(jnp.float32) < size[r:r + 1], row, nb << 12))
    rows.append(jnp.where(place < nb, (place << 12) + place, nb << 12))
    sub = lax.broadcasted_iota(jnp.int32, (16, BLK), 0)
    lane = lax.broadcasted_iota(jnp.int32, (16, BLK), 1)
    sizes = jnp.sum(jnp.where(sub == lane, size, 0.0), axis=0, keepdims=True)
    sizes = jnp.where(lane[:1] == rounds, float(nb), sizes).astype(jnp.int32)
    parts = width // BLK
    for i, row in enumerate(rows):
        for q in range(parts):
            lists[pl.ds(i * parts + q, 1), :] = row[:, q * BLK:(q + 1) * BLK]
    lists[pl.ds(len(rows) * parts, 1), :] = sizes
    for copy in copies[:3]:
        copy.wait()
    lax.fori_loop(0, nb // 8, plane, 0, unroll=4)


def start(positions, normals, strength, near_index, near_count):
    nb, rounds, slots = near_index.shape
    rows = (rounds + 2) * (slots * nb + PAD) // BLK
    vmem = pl.BlockSpec(memory_space=pltpu.VMEM)
    index = near_index.transpose(1, 2, 0)
    args = [positions, normals, strength.reshape(nb, BLK), index, near_count.T]
    msg, lists = pl.pallas_call(
        functools.partial(start_kernel, nb, rounds),
        out_shape=[
            jax.ShapeDtypeStruct((6 * nb, BLK), jnp.float32),
            jax.ShapeDtypeStruct((rows, BLK), jnp.int32),
        ],
        in_specs=[pl.BlockSpec(memory_space=pltpu.HBM)] * 5,
        out_specs=[vmem] * 2,
        scratch_shapes=[pltpu.VMEM(a.shape, a.dtype) for a in args] + [pltpu.SemaphoreType.DMA((5,))],
        compiler_params=pltpu.CompilerParams(vmem_limit_bytes=24 << 20),
        name="start",
    )(*[pltpu.with_memory_space_constraint(a, pltpu.HBM) for a in args])
    return msg, lists.reshape(-1)


def shards(positions, normals, strength, near_index, near_count):
    mine, lists = start(positions, normals, strength, near_index, near_count)
    top_bit = lax.axis_size("bulk").bit_length() - 2
    plan = [("grp", 0), ("grp", 1), ("bulk", 0), ("bulk", 1), ("bulk", 2), ("bulk", top_bit)]
    far = [from_partner(mine, axis, bit) for axis, bit in plan]
    a, tgt, held = phase("own_core", [OWN, 0], lists, [mine, far[0]], [], True)
    b, held = phase("mid", [0, 2, 1, 5], lists, [far[2], far[1], far[5]], [a, tgt, held], True)
    (c,) = phase("end", [5, 3, 4], lists, [far[3], far[4]], [b, tgt, held], False)
    return c.reshape(-1)


def solution(mesh):
    in_specs = (
        P(None, ("bulk", "grp")),
        P(None, ("bulk", "grp")),
        P(("bulk", "grp")),
        P(("bulk", "grp"), None, None),
        P(("bulk", "grp"), None),
    )
    out_specs = P(("bulk", "grp"))
    return jax.shard_map(shards, mesh=mesh, in_specs=in_specs, out_specs=out_specs, check_vma=False)
```
